32 devices in a mesh: dir: 8 (over z, x), coil: 4 (over y, core).
Axes of the slice: x: 2, y: 2, z: 4, core: 2. Of those that a mesh axis runs over, the one named last changes fastest.
Arguments:
- estimate: float32 [48, 2, 90000], P('dir', None, 'coil'), may hold values from -6 to 6
- coil_maps: float32 [16, 2, 1, 300, 300], P('coil'), may hold values from -1 to 1
- kspace: float32 [48, 16, 2, 1, 75, 300], P('dir', 'coil'), may hold values from -6 to 6
- lines: int32 [48, 75], P('dir'), may hold values from 0 to 299, as said below
- first_weight: float32 [48, 2, 96], replicated, may hold values from -0.625 to 0.625
- first_bias: float32 [96], replicated, may hold values from -3 to 3
- second_weight: float32 [96, 48, 2], replicated, may hold values from -0.625 to 0.625
Outputs:
- updated: float32 [48, 2, 90000], P('dir', None, 'coil')
The draws below stay inside these ranges and needn't reach their ends.
Inputs may be any that keep to these rules, and one draw needn't show every extreme that they name: `lines`: the 75 entries of a row are distinct.
All inputs are finite; a program needn't handle non-finite values.
Results may differ from the reference program's by a relative error of at most 0.0003.
Values sent between devices are 32-bit elements; how exact they have to be, the bound alone decides.
No kernel may reach another device: no remote copies, remote signals or barrier semaphores. Data moves between devices by JAX's collectives and lax.ppermute only.
A program may use at most 320 MiB of HBM per device.

```python
import math
import jax
import jax.numpy as jnp
from jax import lax

DIRS = 48
COILS = 16
NY = 300
NX = 300
LINES = 75
CHANNELS = 96
INNER = 2
SLICES = 1
VOX = 90000


def draw_lines(key, part):
    keys = jax.random.split(key, DIRS)

    def one_row(row_key):
        return jax.random.permutation(row_key, NY)[:LINES].astype(jnp.int32)
    return jax.vmap(one_row)(keys)


def shard_levels(key, shape, shards, low, largest):
    gain, own = 1.0, jax.random.fold_in(key, 6)
    for position, shards_of in shards:
        steps = jnp.exp(jax.random.uniform(jax.random.fold_in(own, position), (shards_of,), jnp.float32, low / len(shards), largest / len(shards)))
        gain = gain * jnp.repeat(steps, shape[position] // shards_of).reshape([-1 if axis == position else 1 for axis in range(len(shape))])
    return gain


def bell_draw(key, extent, spread, reach, cuts=(), kind=jnp.bfloat16):
    result = spread * jax.random.normal(key, extent, jnp.float32)
    if cuts:
        result = result * shard_levels(key, extent, cuts, -0.22, 0.18)
    return jnp.clip(result, -reach, reach).astype(kind)


def setup_inputs(seed: int = 0) -> dict:
    splits = jax.random.split(jax.random.key(seed), 8)
    return {
        "estimate": bell_draw(splits[0], (DIRS, 2, VOX), 1.0, 6.0, ((0, 8), (2, 4)), jnp.float32),
        "coil_maps": bell_draw(splits[1], (COILS, 2, SLICES, NY, NX), 0.18, 1.0, ((0, 4),), jnp.float32),
        "kspace": bell_draw(splits[2], (DIRS, COILS, 2, SLICES, LINES, NX), 1.0, 6.0, ((0, 8), (1, 4)), jnp.float32),
        "lines": draw_lines(jax.random.fold_in(splits[7], 71), 0),
        "first_weight": bell_draw(splits[4], (DIRS, 2, CHANNELS), (2 * DIRS) ** -0.5, 0.625, (), jnp.float32),
        "first_bias": bell_draw(splits[5], (CHANNELS,), 0.5, 3.0, (), jnp.float32),
        "second_weight": bell_draw(splits[6], (CHANNELS, DIRS, 2), CHANNELS ** -0.5, 0.625, (), jnp.float32),
    }


def transform_rows(index, length):
    columns = jnp.arange(length, dtype=jnp.int32)
    product = index.astype(jnp.int32)[:, None] * columns[None, :] % length
    angle = 2.0 * math.pi / length * product.astype(jnp.float32)
    scale = 1.0 / math.sqrt(length)
    return (jnp.cos(angle) * scale, -jnp.sin(angle) * scale)

def data_gradient(image, coil_maps, kspace, chosen, cols_cos, cols_sin):
    highest = lax.Precision.HIGHEST
    lines_cos, lines_sin = transform_rows(chosen, NY)
    coil_real, coil_imag = (coil_maps[:, 0], coil_maps[:, 1])
    image_real, image_imag = (image[0][None], image[1][None])
    prod_real = coil_real * image_real - coil_imag * image_imag
    prod_imag = coil_real * image_imag + coil_imag * image_real
    rows_form = 'ly,csyx->cslx'
    half_real = jnp.einsum(rows_form, lines_cos, prod_real, precision=highest) - jnp.einsum(rows_form, lines_sin, prod_imag, precision=highest)
    half_imag = jnp.einsum(rows_form, lines_cos, prod_imag, precision=highest) + jnp.einsum(rows_form, lines_sin, prod_real, precision=highest)
    cols_form = 'cslx,xk->cslk'
    pred_real = jnp.einsum(cols_form, half_real, cols_cos, precision=highest) - jnp.einsum(cols_form, half_imag, cols_sin, precision=highest)
    pred_imag = jnp.einsum(cols_form, half_real, cols_sin, precision=highest) + jnp.einsum(cols_form, half_imag, cols_cos, precision=highest)
    diff_real = pred_real - kspace[:, 0]
    diff_imag = pred_imag - kspace[:, 1]
    back_real = jnp.einsum(cols_form, diff_real, cols_cos, precision=highest) + jnp.einsum(cols_form, diff_imag, cols_sin, precision=highest)
    back_imag = jnp.einsum(cols_form, diff_imag, cols_cos, precision=highest) - jnp.einsum(cols_form, diff_real, cols_sin, precision=highest)
    adjoint_form = 'ly,cslx->csyx'
    spread_real = jnp.einsum(adjoint_form, lines_cos, back_real, precision=highest) + jnp.einsum(adjoint_form, lines_sin, back_imag, precision=highest)
    spread_imag = jnp.einsum(adjoint_form, lines_cos, back_imag, precision=highest) - jnp.einsum(adjoint_form, lines_sin, back_real, precision=highest)
    grad_real = lax.optimization_barrier(jnp.sum(coil_real * spread_real + coil_imag * spread_imag, axis=0))
    grad_imag = lax.optimization_barrier(jnp.sum(coil_real * spread_imag - coil_imag * spread_real, axis=0))
    return jnp.stack([grad_real, grad_imag])

def reference(estimate, coil_maps, kspace, lines, first_weight, first_bias, second_weight):
    highest = lax.Precision.HIGHEST
    cols_cos, cols_sin = transform_rows(jnp.arange(NX, dtype=jnp.int32), NX)
    image = estimate.reshape(DIRS, 2, SLICES, NY, NX)

    def one_direction(item):
        return data_gradient(item[0], coil_maps, item[1], item[2], cols_cos, cols_sin)
    for step in range(INNER):
        gradient = lax.map(one_direction, (image, kspace, lines))
        image = image - 0.5 * gradient
    flat = image.reshape(DIRS, 2, VOX)
    hidden = jnp.einsum('drv,drh->hv', flat, first_weight, precision=highest) + first_bias[:, None]
    hidden = jnp.maximum(hidden, 0.0)
    noise = jnp.einsum('hv,hdr->drv', hidden, second_weight, precision=highest)
    return flat - 0.5 * noise
```

```python
import functools
import math

import jax
import jax.numpy as jnp
import ml_dtypes
import numpy as np
from jax import lax
from jax.experimental import pallas as pl
from jax.experimental.pallas import tpu as pltpu
from jax.sharding import PartitionSpec as P

NY = 300
NX = 300
INNER = 2
SLICES = 1
BF = jnp.bfloat16
F32 = jnp.float32
ROWS = 304
LANES = 384
LPAD = 80
HALF = 150
VMEM_LIMIT = 58 * 2**20


def split_host(table):
    high = table.astype(ml_dtypes.bfloat16)
    low = (table - high.astype(np.float64)).astype(ml_dtypes.bfloat16)
    return high, low


def host_tables():
    index = np.outer(np.arange(NX), np.arange(NX)) % NX
    angle = 2.0 * np.pi / NX * index
    cos, sin = np.cos(angle) / np.sqrt(NX), np.sin(angle) / np.sqrt(NX)
    back = np.zeros((2 * LANES, 2 * LANES))
    back[:NX, :NX] = cos
    back[LANES : LANES + NX, :NX] = -sin
    back[:NX, LANES : LANES + NX] = sin
    back[LANES : LANES + NX, LANES : LANES + NX] = cos
    rows = np.zeros((2, NY, 2 * ROWS))
    rows[0, :, :NY] = cos
    rows[0, :, ROWS : ROWS + NY] = sin
    rows[1, :, :NY] = -sin
    rows[1, :, ROWS : ROWS + NY] = cos
    return back, rows


def split(value):
    high = value.astype(BF)
    return high, (value - high.astype(F32)).astype(BF)


def dot(a, b):
    return lax.dot_general(a, b, (((1,), (0,)), ((), ())), preferred_element_type=F32)


def dot_nt(a, b):
    return lax.dot_general(a, b, (((1,), (1,)), ((), ())), preferred_element_type=F32)


def params():
    return pltpu.CompilerParams(vmem_limit_bytes=VMEM_LIMIT)


def cost(flops, nbytes):
    return pl.CostEstimate(flops=int(flops), bytes_accessed=int(nbytes), transcendentals=0)


def whole(shape):
    return pl.BlockSpec(shape, lambda *_: (0,) * len(shape))


def lines_kernel(lines_ref, rows_hi, rows_lo, cols_hi, cols_lo, w_ref, ah_ref):
    length = lines_ref.shape[1]
    pick = (lines_ref[0] == lax.broadcasted_iota(jnp.int32, (length, NY), 1)).astype(BF)
    for part, (rows, cols) in enumerate(((rows_hi, cols_hi), (rows_lo, cols_lo))):
        for out in range(2):
            at = 2 * LPAD * part + LPAD * out
            w_ref[0, at : at + LPAD, :] = dot(pick, rows[out]).astype(BF)
            block = dot_nt(cols[out], pick).astype(BF)
            if part == 0:
                ah_ref[0, :, LPAD * out : LPAD * out + LPAD] = block
                ah_ref[0, :, 2 * LPAD + LPAD * out : 3 * LPAD + LPAD * out] = block
            else:
                ah_ref[0, :, 4 * LPAD + LPAD * out : 5 * LPAD + LPAD * out] = block


def line_matrices(lines, tables):
    dirs, count = lines.shape
    padded = jnp.pad(lines, ((0, 0), (0, LPAD - count)), constant_values=-1)[:, :, None]
    rows_hi, rows_lo = split_host(tables)
    cols_hi, cols_lo = split_host(tables.transpose(0, 2, 1))
    return pl.pallas_call(
        lines_kernel,
        grid=(dirs,),
        in_specs=[pl.BlockSpec((1, LPAD, 1), lambda d: (d, 0, 0))]
        + [whole((2, NY, 2 * ROWS))] * 2
        + [whole((2, 2 * ROWS, NY))] * 2,
        out_specs=[
            pl.BlockSpec((1, 4 * LPAD, 2 * ROWS), lambda d: (d, 0, 0)),
            pl.BlockSpec((1, 2 * ROWS, 6 * LPAD), lambda d: (d, 0, 0)),
        ],
        out_shape=[
            jax.ShapeDtypeStruct((dirs, 4 * LPAD, 2 * ROWS), BF),
            jax.ShapeDtypeStruct((dirs, 2 * ROWS, 6 * LPAD), BF),
        ],
        compiler_params=params(),
        cost_estimate=cost(6e9, 8e6),
        name="line_matrices",
    )(padded, jnp.asarray(rows_hi), jnp.asarray(rows_lo), jnp.asarray(cols_hi), jnp.asarray(cols_lo))


def maps_kernel(pos_ref, maps_ref, out_ref):
    planes = maps_ref.shape[0]
    for half in range(2):

        @pl.when(pos_ref[0] != half)
        def _():
            for k in range(planes):
                out_ref[:, HALF * k : HALF * (k + 1)] = maps_ref[k, :, HALF * half : HALF * (half + 1)]


def maps_half(pos, maps):
    planes = maps.shape[0]
    return pl.pallas_call(
        maps_kernel,
        grid_spec=pltpu.PrefetchScalarGridSpec(
            num_scalar_prefetch=1,
            grid=(1,),
            in_specs=[whole((planes, NY, NX))],
            out_specs=whole((NY, planes * HALF)),
        ),
        out_shape=jax.ShapeDtypeStruct((NY, planes * HALF), F32),
        compiler_params=params(),
        cost_estimate=cost(1e6, 8e6),
        name="maps_half",
    )(pos, maps)


def estimate_kernel(pos_ref, est_ref, out_ref):
    dirs, _, count = est_ref.shape
    own = dirs // 2
    rows = count // NX
    for half in range(2):
        for group in range(2):
            place = 2 * (pos_ref[0] ^ half) + (pos_ref[1] ^ group)
            for row in range(rows):
                at = NX * row + HALF * half
                out_ref[place, :, :, HALF * row : HALF * (row + 1)] = est_ref[
                    own * group : own * (group + 1), :, at : at + HALF
                ]


def estimate_pieces(pos, estimate):
    dirs, _, count = estimate.shape
    shape = (4, dirs // 2, 2, count // 2)
    return pl.pallas_call(
        estimate_kernel,
        grid_spec=pltpu.PrefetchScalarGridSpec(
            num_scalar_prefetch=1,
            grid=(1,),
            in_specs=[whole(estimate.shape)],
            out_specs=whole(shape),
        ),
        out_shape=jax.ShapeDtypeStruct(shape, F32),
        compiler_params=params(),
        cost_estimate=cost(1e6, 8e6),
        name="estimate_pieces",
    )(pos, estimate)


def back_kernel(base_ref, k_ref, c_ref, f_hi, f_lo, ah_ref, o_ref, kf, xs, ss):
    coils = c_ref.shape[0] // 2
    count = k_ref.shape[2]
    size = coils * LPAD

    @pl.when(pl.program_id(0) == 0)
    def _():
        kf[...] = jnp.zeros_like(kf)

    kf[:, :count, :NX] = k_ref[0]
    for c in range(coils):
        for r in range(2):
            hi, lo = split(kf[2 * c + r])
            xs[LPAD * c : LPAD * (c + 1), LANES * r : LANES * (r + 1)] = hi
            xs[size + LPAD * c : size + LPAD * (c + 1), LANES * r : LANES * (r + 1)] = lo
    t = dot(xs[...], f_hi[...])
    t = t[:size] + t[size:] + dot(xs[:size], f_lo[...])
    for c in range(coils):
        for r in range(2):
            hi, lo = split(t[LPAD * c : LPAD * (c + 1), LANES * r : LANES * (r + 1)])
            lanes = slice(LANES * c, LANES * (c + 1))
            ss[LPAD * r : LPAD * (r + 1), lanes] = hi
            ss[LPAD * (2 + r) : LPAD * (3 + r), lanes] = lo
            ss[LPAD * (4 + r) : LPAD * (5 + r), lanes] = hi
    real, imag = None, None
    for c0 in range(0, coils, 2):
        y = dot(ah_ref[0], ss[:, LANES * c0 : LANES * (c0 + 2)])
        for j in range(2):
            cre, cim = c_ref[2 * (c0 + j)], c_ref[2 * (c0 + j) + 1]
            yre = y[:NY, LANES * j : LANES * j + NX]
            yim = y[ROWS : ROWS + NY, LANES * j : LANES * j + NX]
            tre, tim = cre * yre + cim * yim, cre * yim - cim * yre
            real = tre if real is None else real + tre
            imag = tim if imag is None else imag + tim
    o_ref[0, 0] = real
    o_ref[0, 1] = imag


def back_partial(base, dirs, kspace, maps, f_hi, f_lo, ah, name):
    planes = maps.shape[0]
    count = kspace.shape[2]
    size = planes // 2 * LPAD
    return pl.pallas_call(
        back_kernel,
        grid_spec=pltpu.PrefetchScalarGridSpec(
            num_scalar_prefetch=1,
            grid=(dirs,),
            in_specs=[
                pl.BlockSpec((1, planes, count, NX), lambda d, s: (s[0] + d, 0, 0, 0)),
                whole((planes, NY, NX)),
                whole((2 * LANES, 2 * LANES)),
                whole((2 * LANES, 2 * LANES)),
                pl.BlockSpec((1, 2 * ROWS, 6 * LPAD), lambda d, s: (s[0] + d, 0, 0)),
            ],
            out_specs=pl.BlockSpec((1, 2, NY, NX), lambda d, s: (d, 0, 0, 0)),
            scratch_shapes=[
                pltpu.VMEM((planes, LPAD, LANES), F32),
                pltpu.VMEM((2 * size, 2 * LANES), BF),
                pltpu.VMEM((6 * LPAD, planes // 2 * LANES), BF),
            ],
        ),
        out_shape=jax.ShapeDtypeStruct((dirs, 2, NY, NX), F32),
        compiler_params=params(),
        cost_estimate=cost(9e9, 12e6),
        name=name,
    )(base, kspace, maps, f_hi, f_lo, ah)


def halves_kernel(pos_ref, a_ref, b_ref, keep_ref, send_ref):
    planes = 2 * a_ref.shape[0]
    for half in range(2):
        for k in range(planes):
            lanes = slice(HALF * half, HALF * (half + 1))
            total = a_ref[k // 2, k % 2, :, lanes] + b_ref[k // 2, k % 2, :, lanes]
            place = slice(HALF * k, HALF * (k + 1))

            @pl.when(pos_ref[0] == half)
            def _():
                keep_ref[:, place] = total

            @pl.when(pos_ref[0] != half)
            def _():
                send_ref[:, place] = total


def back_halves(pos, a, b):
    shape = (NY, 2 * a.shape[0] * HALF)
    return pl.pallas_call(
        halves_kernel,
        grid_spec=pltpu.PrefetchScalarGridSpec(
            num_scalar_prefetch=1,
            grid=(1,),
            in_specs=[whole(a.shape)] * 2,
            out_specs=[whole(shape)] * 2,
        ),
        out_shape=[jax.ShapeDtypeStruct(shape, F32)] * 2,
        compiler_params=params(),
        cost_estimate=cost(1e6, 10e6),
        name="back_halves",
    )(pos, a, b)


def normal(pairs, zs, w_ref, ah_ref, xs, ss, acc):
    groups = pairs.shape[0] // 4
    acc[...] = jnp.zeros_like(acc)

    def group(g, carry):
        for j in range(2):
            cre, cim = pairs[4 * g + 2 * j], pairs[4 * g + 2 * j + 1]
            zre, zim = zs[0], zs[1]
            lanes = slice(LANES * j, LANES * (j + 1))
            hi, lo = split(cre * zre - cim * zim)
            xs[:ROWS, lanes] = hi
            xs[2 * ROWS : 3 * ROWS, lanes] = lo
            hi, lo = split(cre * zim + cim * zre)
            xs[ROWS : 2 * ROWS, lanes] = hi
            xs[3 * ROWS :, lanes] = lo
        size = 2 * LPAD
        t = dot(w_ref[0], xs[: 2 * ROWS])
        t = t[:size] + t[size:] + dot(w_ref[0, :size], xs[2 * ROWS :])
        hi, lo = split(t)
        ss[:size] = hi
        ss[size : 2 * size] = lo
        ss[2 * size :] = hi
        y = dot(ah_ref[0], ss[...])
        for j in range(2):
            cre, cim = pairs[4 * g + 2 * j], pairs[4 * g + 2 * j + 1]
            yre = y[:ROWS, LANES * j : LANES * (j + 1)]
            yim = y[ROWS:, LANES * j : LANES * (j + 1)]
            acc[0] += cre * yre + cim * yim
            acc[1] += cre * yim - cim * yre
        return carry

    lax.fori_loop(0, groups, group, 0)


def first_kernel(pos_ref, base_ref, own_ref, mate_ref, got_ref, gotm_ref, e0, e1, e2, e3, w_ref, ah_ref,
                 u_ref, pairs, zs, zf, xs, ss, acc):
    planes = own_ref.shape[0]
    count = e0.shape[2]
    rows = count // HALF
    d = pl.program_id(0)

    @pl.when(d == 0)
    def _():
        pairs[...] = jnp.zeros_like(pairs)
        zs[...] = jnp.zeros_like(zs)
        for part, (src, got) in enumerate(((own_ref, got_ref), (mate_ref, gotm_ref))):
            for k in range(planes):
                for half in range(2):

                    @pl.when(pos_ref[0] == half)
                    def _():
                        pairs[planes * part + k, :NY, :HALF] = src[k, :, HALF * half : HALF * (half + 1)]

                pairs[planes * part + k, :NY, HALF : 2 * HALF] = got[:, HALF * k : HALF * (k + 1)]

    for k, piece in enumerate((e0, e1, e2, e3)):
        start = rows * ((2 * pos_ref[0] + pos_ref[1]) ^ k)
        for row in range(rows):
            seg = piece[0, :, HALF * row : HALF * (row + 1)]
            for r in range(2):
                zf[r, pl.ds(start + row, 1), :] = seg[r : r + 1]
    for r in range(2):
        zs[r, :NY, :HALF] = zf[r, :NY, :]
        zs[r, :NY, HALF : 2 * HALF] = zf[r, :NY, :]
    normal(pairs, zs, w_ref, ah_ref, xs, ss, acc)
    for r in range(2):
        u_ref[0, r] = zs[r, :NY, :HALF] - 0.5 * (acc[r, :NY, :HALF] + acc[r, :NY, HALF : 2 * HALF])


def pair_scratch(planes):
    return [
        pltpu.VMEM((2, ROWS, LANES), F32),
        pltpu.VMEM((2, ROWS, HALF), F32),
        pltpu.VMEM((4 * ROWS, 2 * LANES), BF),
        pltpu.VMEM((6 * LPAD, 2 * LANES), BF),
        pltpu.VMEM((2, ROWS, LANES), F32),
    ]


def line_specs():
    return [
        pl.BlockSpec((1, 4 * LPAD, 2 * ROWS), lambda d, p, s: (s[0] + d, 0, 0)),
        pl.BlockSpec((1, 2 * ROWS, 6 * LPAD), lambda d, p, s: (s[0] + d, 0, 0)),
    ]


def first_step(pos, base, own, mate, got, gotm, pieces, w, ah):
    planes = own.shape[0]
    dirs, _, count = pieces[0].shape
    piece = pl.BlockSpec((1, 2, count), lambda d, p, s: (d, 0, 0))
    return pl.pallas_call(
        first_kernel,
        grid_spec=pltpu.PrefetchScalarGridSpec(
            num_scalar_prefetch=2,
            grid=(dirs,),
            in_specs=[whole(own.shape)] * 2 + [whole(got.shape)] * 2 + [piece] * 4 + line_specs(),
            out_specs=[
                pl.BlockSpec((1, 2, NY, HALF), lambda d, p, s: (d, 0, 0, 0)),
                whole((2 * planes, ROWS, LANES)),
            ],
            scratch_shapes=pair_scratch(planes),
        ),
        out_shape=[
            jax.ShapeDtypeStruct((dirs, 2, NY, HALF), F32),
            jax.ShapeDtypeStruct((2 * planes, ROWS, LANES), F32),
        ],
        compiler_params=params(),
        cost_estimate=cost(18e9, 20e6),
        name="first_step",
    )(pos, base, own, mate, got, gotm, *pieces, w, ah)


def second_kernel(pos_ref, base_ref, u_ref, keep_ref, got_ref, pairs, w_ref, ah_ref, z_ref, zs, zf, xs, ss, acc):
    d = pl.program_id(0)

    @pl.when(d == 0)
    def _():
        zs[...] = jnp.zeros_like(zs)

    for k in range(keep_ref.shape[1] // (2 * HALF)):

        @pl.when(d == k)
        def _():
            for r in range(2):
                lanes = slice(HALF * (2 * k + r), HALF * (2 * k + r + 1))
                zf[r, :NY, :] = 0.5 * (keep_ref[:, lanes] + got_ref[:, lanes])

    for r in range(2):
        z = u_ref[0, r] + zf[r, :NY, :]
        zs[r, :NY, :HALF] = z
        zs[r, :NY, HALF : 2 * HALF] = z
    normal(pairs, zs, w_ref, ah_ref, xs, ss, acc)
    for r in range(2):
        total = 0.5 * (acc[r, :NY, :HALF] + acc[r, :NY, HALF : 2 * HALF])
        z_ref[0, r] = zs[r, :NY, :HALF] + zf[r, :NY, :] - total


def second_step(pos, base, u, keep, got, pairs, w, ah):
    dirs = u.shape[0]
    plane = pl.BlockSpec((1, 2, NY, HALF), lambda d, p, s: (d, 0, 0, 0))
    return pl.pallas_call(
        second_kernel,
        grid_spec=pltpu.PrefetchScalarGridSpec(
            num_scalar_prefetch=2,
            grid=(dirs,),
            in_specs=[plane] + [whole(keep.shape)] * 2 + [whole(pairs.shape)] + line_specs(),
            out_specs=plane,
            scratch_shapes=pair_scratch(pairs.shape[0] // 2),
        ),
        out_shape=jax.ShapeDtypeStruct(u.shape, F32),
        compiler_params=params(),
        cost_estimate=cost(18e9, 20e6),
        name="second_step",
    )(pos, base, u, keep, got, pairs, w, ah)


def chunk_size(dirs):
    return -(-(75 * HALF) // (dirs * 128)) * 128


def flat_kernel(size, z_ref, o_ref, flat):
    dirs = z_ref.shape[0]
    rows = NY // 4
    parts = o_ref.shape[0] // 4
    for p in range(4):
        for row in range(rows):
            for d in range(dirs):
                for r in range(2):
                    flat[d, r : r + 1, HALF * row : HALF * (row + 1)] = z_ref[d, r, rows * p + row : rows * p + row + 1, :]
        for q in range(parts):
            o_ref[4 * q + p] = flat[:, :, size * q : size * (q + 1)]


def flat_chunks(z, parts):
    dirs = z.shape[0]
    size = chunk_size(parts)
    shape = (4 * parts, dirs, 2, size)
    return pl.pallas_call(
        functools.partial(flat_kernel, size),
        grid=(1,),
        in_specs=[whole(z.shape)],
        out_specs=whole(shape),
        out_shape=jax.ShapeDtypeStruct(shape, F32),
        scratch_shapes=[pltpu.VMEM((dirs, 2, size * parts), F32)],
        compiler_params=params(),
        cost_estimate=cost(1e6, 5e6),
        name="flat_chunks",
    )(z)


def denoise_kernel(x_ref, w1_ref, b1_ref, w2_ref, o_ref, xs):
    parts = x_ref.shape[0] // 4
    own, size = x_ref.shape[1], x_ref.shape[3]
    for q in range(parts):
        for y in range(2):
            for core in range(2):
                for d in range(own):
                    at = 4 * own * q + 2 * own * core + 2 * d
                    xs[at : at + 2, size * y : size * (y + 1)] = x_ref[4 * q + 2 * y + core, d]
    w1h, w1l = split(w1_ref[...])
    w2h, w2l = split(w2_ref[...])
    w1 = jnp.concatenate([w1h, w1h, w1l], axis=1)
    w2 = jnp.concatenate([w2h, w2h, w2l], axis=1)
    x = xs[...]
    hi, lo = split(x)
    hidden = dot(w1, jnp.concatenate([hi, lo, hi], axis=0)) + b1_ref[...]
    hi, lo = split(jnp.maximum(hidden, 0.0))
    noise = dot(w2, jnp.concatenate([hi, lo, hi], axis=0))
    xs[...] = x - 0.5 * noise
    for q in range(parts):
        for d in range(2 * own):
            at = 4 * own * q + 2 * d
            o_ref[q, d] = xs[at : at + 2, :]


def denoise(x, w1, b1, w2):
    parts, own, size = x.shape[0] // 4, x.shape[1], x.shape[3]
    shape = (parts, 2 * own, 2, 2 * size)
    return pl.pallas_call(
        denoise_kernel,
        grid=(1,),
        in_specs=[whole(x.shape), whole(w1.shape), whole(b1.shape), whole(w2.shape)],
        out_specs=whole(shape),
        out_shape=jax.ShapeDtypeStruct(shape, F32),
        scratch_shapes=[pltpu.VMEM((4 * own * parts, 2 * size), F32)],
        compiler_params=params(),
        cost_estimate=cost(1e9, 3e6),
        name="denoise",
    )(x, w1, b1, w2)


def rows_kernel(x_ref, o_ref, flat):
    parts, size = x_ref.shape[0], x_ref.shape[3] // 2
    rows = o_ref.shape[2] // NX
    for half in range(2):
        for q in range(parts):
            flat[:, :, size * q : size * (q + 1)] = x_ref[q, :, :, size * half : size * (half + 1)]
        for row in range(rows):
            at = NX * row + HALF * half
            o_ref[:, :, at : at + HALF] = flat[:, :, HALF * row : HALF * (row + 1)]


def flat_rows(x, count):
    parts, dirs, _, size = x.shape
    return pl.pallas_call(
        rows_kernel,
        grid=(1,),
        in_specs=[whole(x.shape)],
        out_specs=whole((dirs, 2, count)),
        out_shape=jax.ShapeDtypeStruct((dirs, 2, count), F32),
        scratch_shapes=[pltpu.VMEM((dirs, 2, parts * size // 2), F32)],
        compiler_params=params(),
        cost_estimate=cost(1e6, 3e6),
        name="flat_rows",
    )(x)


def paired(estimate, coil_maps, kspace, lines, first_weight, first_bias, second_weight):
    dirs, _, share = estimate.shape
    own_dirs = dirs // 2
    coils = coil_maps.shape[0]
    parts = lax.axis_size("dir")
    back, rows = host_tables()
    f_hi, f_lo = (jnp.asarray(t) for t in split_host(back))
    index = lax.axis_index("coil")
    pos = jnp.stack([index // 2, index % 2]).astype(jnp.int32)
    mine = (own_dirs * pos[1:2]).astype(jnp.int32)
    other = (own_dirs * (1 - pos[1:2])).astype(jnp.int32)

    def swap(value, k):
        return lax.ppermute(value, "coil", [(p, p ^ k) for p in range(4)])

    maps = coil_maps.reshape(2 * coils, NY, NX)
    mate = swap(maps, 1)
    got = swap(maps_half(pos, maps), 2)
    gotm = swap(got, 1)
    pieces = estimate_pieces(pos, estimate)
    pieces = [pieces[k] if k == 0 else swap(pieces[k], k) for k in range(4)]
    w, ah = line_matrices(lines, rows)
    flat_k = kspace.reshape(dirs, 2 * coils, kspace.shape[4], NX)
    theirs = swap(back_partial(other, own_dirs, flat_k, maps, f_hi, f_lo, ah, "back_other"), 1)
    ours = back_partial(mine, own_dirs, flat_k, maps, f_hi, f_lo, ah, "back_own")
    keep, send = back_halves(pos, ours, theirs)
    got_b = swap(send, 2)
    u, pairs = first_step(pos, mine, maps, mate, got, gotm, pieces, w, ah)
    z = second_step(pos, mine, u, keep, got_b, pairs, w, ah)
    chunks = flat_chunks(z, parts)
    received = lax.all_to_all(chunks, ("dir", "coil"), split_axis=0, concat_axis=0, tiled=True)
    channels = first_bias.shape[0]
    w1 = first_weight.reshape(-1, channels).T
    w2 = second_weight.reshape(channels, -1).T
    result = denoise(received, w1, first_bias[:, None], w2)
    returned = lax.all_to_all(result, "dir", split_axis=0, concat_axis=0, tiled=True)
    return flat_rows(returned, share)


def transform_rows(index, length):
    columns = jnp.arange(length, dtype=jnp.int32)
    product = index[:, None] * columns[None, :] % length
    angle = 2.0 * math.pi / length * product.astype(jnp.float32)
    scale = 1.0 / math.sqrt(length)
    return (jnp.cos(angle) * scale, -jnp.sin(angle) * scale)


def data_gradient(image, coil_maps, kspace, chosen, cols_cos, cols_sin):
    highest = lax.Precision.HIGHEST
    lines_cos, lines_sin = transform_rows(chosen, NY)
    coil_real, coil_imag = (coil_maps[:, 0], coil_maps[:, 1])
    image_real, image_imag = (image[0][None], image[1][None])
    prod_real = coil_real * image_real - coil_imag * image_imag
    prod_imag = coil_real * image_imag + coil_imag * image_real
    rows_form = "ly,csyx->cslx"
    half_real = jnp.einsum(rows_form, lines_cos, prod_real, precision=highest) - jnp.einsum(
        rows_form, lines_sin, prod_imag, precision=highest
    )
    half_imag = jnp.einsum(rows_form, lines_cos, prod_imag, precision=highest) + jnp.einsum(
        rows_form, lines_sin, prod_real, precision=highest
    )
    cols_form = "cslx,xk->cslk"
    pred_real = jnp.einsum(cols_form, half_real, cols_cos, precision=highest) - jnp.einsum(
        cols_form, half_imag, cols_sin, precision=highest
    )
    pred_imag = jnp.einsum(cols_form, half_real, cols_sin, precision=highest) + jnp.einsum(
        cols_form, half_imag, cols_cos, precision=highest
    )
    diff_real = pred_real - kspace[:, 0]
    diff_imag = pred_imag - kspace[:, 1]
    back_real = jnp.einsum(cols_form, diff_real, cols_cos, precision=highest) + jnp.einsum(
        cols_form, diff_imag, cols_sin, precision=highest
    )
    back_imag = jnp.einsum(cols_form, diff_imag, cols_cos, precision=highest) - jnp.einsum(
        cols_form, diff_real, cols_sin, precision=highest
    )
    adjoint_form = "ly,cslx->csyx"
    spread_real = jnp.einsum(adjoint_form, lines_cos, back_real, precision=highest) + jnp.einsum(
        adjoint_form, lines_sin, back_imag, precision=highest
    )
    spread_imag = jnp.einsum(adjoint_form, lines_cos, back_imag, precision=highest) - jnp.einsum(
        adjoint_form, lines_sin, back_real, precision=highest
    )
    grad_real = jnp.sum(coil_real * spread_real + coil_imag * spread_imag, axis=0)
    grad_imag = jnp.sum(coil_real * spread_imag - coil_imag * spread_real, axis=0)
    return jnp.stack([grad_real, grad_imag])


def per_device(estimate, coil_maps, kspace, lines, first_weight, first_bias, second_weight):
    highest = lax.Precision.HIGHEST
    dir_local = estimate.shape[0]
    share = estimate.shape[2]
    voxels = SLICES * NY * NX
    cols_cos, cols_sin = transform_rows(jnp.arange(NX, dtype=jnp.int32), NX)
    whole = lax.all_gather(estimate, "coil", axis=2, tiled=True)
    position = lax.axis_index("coil")
    current = whole
    for step in range(INNER):
        image = current.reshape(dir_local, 2, SLICES, NY, NX)

        def one_direction(item):
            return data_gradient(item[0], coil_maps, item[1], item[2], cols_cos, cols_sin)

        terms = lax.map(one_direction, (image, kspace, lines))
        total = lax.psum(terms.reshape(dir_local, 2, voxels), "coil")
        current = current - 0.5 * total
    own = lax.dynamic_slice_in_dim(current, position * share, share, 2)
    groups = lax.axis_size("dir")
    padded_len = -(-share // groups) * groups
    padded = jnp.pad(own, ((0, 0), (0, 0), (0, padded_len - share)))
    gathered = lax.all_to_all(padded, "dir", split_axis=2, concat_axis=0, tiled=True)
    hidden = (
        jnp.einsum("drv,drh->hv", gathered, first_weight, precision=highest) + first_bias[:, None]
    )
    hidden = jnp.maximum(hidden, 0.0)
    noise = jnp.einsum("hv,hdr->drv", hidden, second_weight, precision=highest)
    returned = lax.all_to_all(noise, "dir", split_axis=0, concat_axis=2, tiled=True)
    return own - 0.5 * returned[:, :, :share]


def chosen(*arrays):
    estimate, coil_maps, kspace = arrays[:3]
    fits = (
        lax.axis_size("coil") == 4
        and estimate.shape[0] % 2 == 0
        and estimate.shape[2] * 4 == NY * NX
        and coil_maps.shape[0] % 2 == 0
        and kspace.shape[4] <= LPAD
    )
    return paired(*arrays) if fits else per_device(*arrays)


def solution(mesh):
    return jax.shard_map(
        chosen,
        mesh=mesh,
        in_specs=(
            P("dir", None, "coil"),
            P("coil", None, None, None, None),
            P("dir", "coil", None, None, None, None),
            P("dir", None),
            P(),
            P(),
            P(),
        ),
        out_specs=P("dir", None, "coil"),
        check_vma=False,
    )
```

```python
import functools
import math

import jax
import jax.numpy as jnp
import ml_dtypes
import numpy as np
from jax import lax
from jax.experimental import pallas as pl
from jax.experimental.pallas import tpu as pltpu
from jax.sharding import PartitionSpec as P

NY = 300
NX = 300
INNER = 2
SLICES = 1
BF = jnp.bfloat16
F32 = jnp.float32
FOLD = 160
LINK = 152
ROWS = 2 * FOLD
LANES = 384
LPAD = 80
HALF = 150
BACK = 256
GROUP = 4


def split_host(table):
    high = table.astype(ml_dtypes.bfloat16)
    low = (table - high.astype(np.float64)).astype(ml_dtypes.bfloat16)
    return high, low


def host_tables():
    index = np.outer(np.arange(NX), np.arange(NX)) % NX
    angle = 2.0 * np.pi / NX * index
    cos, sin = np.cos(angle) / np.sqrt(NX), np.sin(angle) / np.sqrt(NX)
    back = np.zeros((2 * LANES, 2 * LANES))
    back[:NX, :NX] = cos
    back[LANES : LANES + NX, :NX] = -sin
    back[:NX, LANES : LANES + NX] = sin
    back[LANES : LANES + NX, LANES : LANES + NX] = cos
    rows = np.zeros((NY, ROWS))
    rows[:, : NY // 2 + 1] = cos[:, : NY // 2 + 1]
    rows[:, FOLD : FOLD + NY // 2] = sin[:, : NY // 2]
    return back, rows


def folded(row):
    return row if row <= NY // 2 else FOLD + NY - row


def split(value):
    high = value.astype(BF)
    return high, (value - high.astype(F32)).astype(BF)


def dot(a, b):
    return lax.dot_general(a, b, (((1,), (0,)), ((), ())), preferred_element_type=F32)


def dot_high(a, b, contract=(1, 0), precision=lax.Precision.HIGH):
    dims = (((contract[0],), (contract[1],)), ((), ()))
    return lax.dot_general(a, b, dims, precision=precision, preferred_element_type=F32)


def params(mib):
    return pltpu.CompilerParams(vmem_limit_bytes=mib * 2**20)


def cost(flops, nbytes):
    return pl.CostEstimate(flops=int(flops / 1000), bytes_accessed=int(nbytes / 1000), transcendentals=0)


def result(shape):
    return pl.BlockSpec(shape, lambda *_: (0,) * len(shape))


def whole(shape):
    return pl.BlockSpec(shape, lambda *_: (0,) * len(shape), pipeline_mode=pl.Buffered(1))


def lines_kernel(lines_ref, rows_ref, cols_ref, w_ref, ah_ref):
    pick = (lines_ref[0] == lax.broadcasted_iota(jnp.int32, (LPAD, NY), 1)).astype(F32)
    w_ref[0] = dot_high(pick, rows_ref[...], precision=lax.Precision.HIGHEST)
    hi, lo = split(dot_high(cols_ref[...], pick, (1, 1), precision=lax.Precision.HIGHEST))
    ah_ref[0] = jnp.concatenate(
        [v.astype(F32) for v in (hi, hi, lo)] + [jnp.zeros((ROWS, BACK - 3 * LPAD), F32)], axis=1
    ).astype(BF)


def line_matrices(lines, table):
    dirs, count = lines.shape
    padded = jnp.pad(lines, ((0, 0), (0, LPAD - count)), constant_values=-1)[:, :, None]
    tables = [jnp.asarray(t, F32) for t in (table, table.T)]
    return pl.pallas_call(
        lines_kernel,
        grid=(dirs,),
        in_specs=[pl.BlockSpec((1, LPAD, 1), lambda d: (d, 0, 0))] + [whole(t.shape) for t in tables],
        out_specs=[
            pl.BlockSpec((1, LPAD, ROWS), lambda d: (d, 0, 0)),
            pl.BlockSpec((1, ROWS, BACK), lambda d: (d, 0, 0)),
        ],
        out_shape=[
            jax.ShapeDtypeStruct((dirs, LPAD, ROWS), F32),
            jax.ShapeDtypeStruct((dirs, ROWS, BACK), BF),
        ],
        compiler_params=params(16),
        cost_estimate=cost(1e9, 1e6),
        name="line_matrices",
    )(padded, *tables)


def maps_kernel(pos_ref, maps_ref, out_ref, send_ref):
    planes = maps_ref.shape[0]
    mirror = FOLD + NY // 2
    send_ref[...] = jnp.zeros_like(send_ref)

    @pl.loop(0, planes)
    def _(k):
        out_ref[k] = jnp.zeros_like(out_ref[k])
        for row in range(NY):
            out_ref[k, folded(row), :NX] = maps_ref[k, row, 0, :]

    for half in range(2):

        @pl.when(pos_ref[0] != half)
        def _():
            for k in range(planes):
                for part in range(2):
                    send_ref[LINK * part : LINK * (part + 1), HALF * k : HALF * (k + 1)] = out_ref[
                        k, FOLD * part : FOLD * part + LINK, HALF * half : HALF * (half + 1)
                    ]


def folded_maps(pos, maps):
    planes = maps.shape[0]
    shapes = [(planes, ROWS, LANES), (2 * LINK, planes * HALF)]
    return pl.pallas_call(
        maps_kernel,
        grid_spec=pltpu.PrefetchScalarGridSpec(
            num_scalar_prefetch=1,
            grid=(1,),
            in_specs=[whole(maps.shape)],
            out_specs=[result(s) for s in shapes],
        ),
        out_shape=[jax.ShapeDtypeStruct(s, F32) for s in shapes],
        compiler_params=params(24),
        cost_estimate=cost(1e6, 12e6),
        name="folded_maps",
    )(pos, maps)


def estimate_kernel(pos_ref, est_ref, *out_refs):
    dirs, _, count = est_ref.shape
    own = dirs // 2
    rows = count // NX
    for y in range(2):

        @pl.when(pos_ref[0] == y)
        def _():
            for k, out_ref in enumerate(out_refs):
                group = pl.ds(own * (pos_ref[1] ^ (k % 2)), own)
                for row in range(rows):
                    at = NX * row + HALF * (y ^ (k // 2))
                    out_ref[:, :, HALF * row : HALF * (row + 1)] = est_ref[group, :, at : at + HALF]


def estimate_pieces(pos, estimate):
    dirs, _, count = estimate.shape
    shape = (dirs // 2, 2, count // 2)
    return pl.pallas_call(
        estimate_kernel,
        grid_spec=pltpu.PrefetchScalarGridSpec(
            num_scalar_prefetch=1,
            grid=(1,),
            in_specs=[whole(estimate.shape)],
            out_specs=[result(shape)] * 4,
        ),
        out_shape=[jax.ShapeDtypeStruct(shape, F32)] * 4,
        compiler_params=params(16),
        cost_estimate=cost(1e6, 8e6),
        name="estimate_pieces",
    )(pos, estimate)


def adjoint(y, j, rows):
    re, im = slice(2 * LANES * j, 2 * LANES * j + LANES), slice(2 * LANES * j + LANES, 2 * LANES * (j + 1))
    mirror = pl.ds(FOLD + rows.start, rows.size)
    ure, uim, vre, vim = y[rows, re], y[rows, im], y[mirror, re], y[mirror, im]
    return ((rows, ure - vim, uim + vre), (mirror, ure + vim, uim - vre))


def back_kernel(base_ref, pos_ref, k0_ref, k1_ref, c0_ref, c1_ref, f_ref, ah_ref, keep_ref, send_ref, xs, ts, ss, ys, bs):
    coils = c0_ref.shape[0] // 2
    count = k0_ref.shape[2]
    wide = 2 * LANES
    sources = [(k, m, c) for k, m in ((k0_ref, c0_ref), (k1_ref, c1_ref)) for c in range(coils)]

    @pl.when(pl.program_id(0) == 0)
    def _():
        xs[...] = jnp.zeros_like(xs)
        ss[...] = jnp.zeros_like(ss)

    for part, k_ref in enumerate((k0_ref, k1_ref)):

        @pl.loop(0, coils)
        def _(c):
            base = pl.multiple_of(LPAD * (coils * part + c), LPAD)
            for r in range(2):
                xs[pl.ds(base, count), LANES * r : LANES * r + NX] = k_ref[0, 2 * c + r, :, 0, :]

    hi, lo = split(xs[...])
    ts[...] = dot(hi, f_ref[:wide]) + dot(lo, f_ref[:wide]) + dot(hi, f_ref[wide:])

    @pl.loop(0, LPAD // 16)
    def _(i):
        at = pl.multiple_of(16 * i, 16)
        for c in range(len(sources)):
            for lane in range(0, wide, 256):
                hi, lo = split(ts[pl.ds(LPAD * c + at, 16), lane : lane + 256])
                lanes = slice(wide * c + lane, wide * c + lane + 256)
                ss[pl.ds(at, 16), lanes] = hi
                ss[pl.ds(LPAD + at, 16), lanes] = lo
                ss[pl.ds(2 * LPAD + at, 16), lanes] = hi

    ys[...] = dot(ah_ref[0], ss[...])

    @pl.loop(0, FOLD // 8)
    def _(i):
        rows = pl.ds(pl.multiple_of(8 * i, 8), 8)
        sums = [None] * 4
        for place, (_, c_ref, c) in enumerate(sources):
            for part, (at, yre, yim) in enumerate(adjoint(ys, place, rows)):
                cre, cim = c_ref[2 * c, at], c_ref[2 * c + 1, at]
                for r, term in enumerate((cre * yre + cim * yim, cre * yim - cim * yre)):
                    old = sums[2 * part + r]
                    sums[2 * part + r] = term if old is None else old + term
        for part in range(2):
            for r in range(2):
                bs[r, pl.ds(pl.multiple_of(FOLD * part + 8 * i, 8), 8), :] = sums[2 * part + r]

    for half in range(2):
        lanes = slice(HALF * half, HALF * (half + 1))

        @pl.when(pos_ref[0] == half)
        def _():
            for r in range(2):
                keep_ref[0, r] = bs[r, :, lanes]

        for k in range(send_ref.shape[1] // (2 * HALF)):

            @pl.when((pos_ref[0] != half) & (pl.program_id(0) == k))
            def _():
                for r in range(2):
                    place = slice(HALF * (2 * k + r), HALF * (2 * k + r + 1))
                    for part in range(2):
                        send_ref[LINK * part : LINK * (part + 1), place] = bs[
                            r, FOLD * part : FOLD * part + LINK, lanes
                        ]


def back_sums(base, pos, dirs, k_own, k_mate, own, mate, f_back, ah):
    _, planes, count, _, _ = k_own.shape
    link = (2 * LINK, 2 * dirs * HALF)
    k_spec = pl.BlockSpec((1, planes, count, 1, NX), lambda d, s, *_: (s[0] + d, 0, 0, 0, 0))
    return pl.pallas_call(
        back_kernel,
        grid_spec=pltpu.PrefetchScalarGridSpec(
            num_scalar_prefetch=2,
            grid=(dirs,),
            in_specs=[k_spec] * 2
            + [whole((planes, ROWS, LANES))] * 2
            + [whole(f_back.shape), pl.BlockSpec((1, ROWS, BACK), lambda d, s, *_: (s[0] + d, 0, 0))],
            out_specs=[pl.BlockSpec((1, 2, ROWS, HALF), lambda d, *_: (d, 0, 0, 0)), result(link)],
            scratch_shapes=[
                pltpu.VMEM((planes * LPAD, 2 * LANES), F32),
                pltpu.VMEM((planes * LPAD, 2 * LANES), F32),
                pltpu.VMEM((BACK, 2 * planes * LANES), BF),
                pltpu.VMEM((ROWS, 2 * planes * LANES), F32),
                pltpu.VMEM((2, ROWS, LANES), F32),
            ],
        ),
        out_shape=[jax.ShapeDtypeStruct((dirs, 2, ROWS, HALF), F32), jax.ShapeDtypeStruct(link, F32)],
        compiler_params=params(48),
        cost_estimate=cost(14e9, 22e6),
        name="back_sums",
    )(base, pos, k_own, k_mate, own, mate, f_back, ah)


def normal(pairs, zs, w_ref, ah_ref, xs, ts, ss, ys, acc):
    groups = pairs.shape[0] // (2 * GROUP)
    wide = 2 * LANES

    @pl.loop(0, groups)
    def _(g):
        @pl.loop(0, FOLD // 16)
        def _(i):
            at = pl.multiple_of(16 * i, 16)
            rows = (pl.ds(at, 16), pl.ds(FOLD + at, 16))
            for lane in range(0, LANES, 128):
                lanes = slice(lane, lane + 128)
                z = [(zs[0, r, lanes], zs[1, r, lanes]) for r in rows]
                for j in range(GROUP):
                    p = 2 * (GROUP * g + j)
                    parts = []
                    for (zre, zim), r in zip(z, rows):
                        cre, cim = pairs[p, r, lanes], pairs[p + 1, r, lanes]
                        parts.append((cre * zre - cim * zim, cre * zim + cim * zre))
                    (re1, im1), (re2, im2) = parts
                    place = wide * j + lane
                    for put, even, odd in ((place, re1 + re2, im1 - im2), (place + LANES, im1 + im2, re2 - re1)):
                        for base, value in ((0, even), (FOLD, odd)):
                            xs[pl.ds(base + at, 16), put : put + 128] = value

        ts[...] = dot_high(w_ref[0], xs[...])

        @pl.loop(0, LPAD // 16)
        def _(i):
            at = pl.multiple_of(16 * i, 16)
            for lane in range(0, GROUP * wide, 256):
                lanes = slice(lane, lane + 256)
                hi, lo = split(ts[pl.ds(at, 16), lanes])
                ss[pl.ds(at, 16), lanes] = hi
                ss[pl.ds(LPAD + at, 16), lanes] = lo
                ss[pl.ds(2 * LPAD + at, 16), lanes] = hi

        ys[...] = dot(ah_ref[0], ss[...])

        @pl.loop(0, FOLD // 8)
        def _(i):
            at = pl.multiple_of(8 * i, 8)
            rows = (pl.ds(at, 8), pl.ds(FOLD + at, 8))
            for lane in range(0, LANES, 128):
                lanes = slice(lane, lane + 128)
                sums = [None] * 4
                for j in range(GROUP):
                    p = 2 * (GROUP * g + j)
                    re = slice(wide * j + lane, wide * j + lane + 128)
                    im = slice(wide * j + LANES + lane, wide * j + LANES + lane + 128)
                    ure, uim, vre, vim = ys[rows[0], re], ys[rows[0], im], ys[rows[1], re], ys[rows[1], im]
                    for part, (yre, yim) in enumerate(((ure - vim, uim + vre), (ure + vim, uim - vre))):
                        cre, cim = pairs[p, rows[part], lanes], pairs[p + 1, rows[part], lanes]
                        for r, term in enumerate((cre * yre + cim * yim, cre * yim - cim * yre)):
                            old = sums[2 * part + r]
                            sums[2 * part + r] = term if old is None else old + term
                for part in range(2):
                    for r in range(2):
                        value = sums[2 * part + r]
                        acc[r, rows[part], lanes] = value + jnp.where(g > 0, acc[r, rows[part], lanes], 0.0)


def clear(*refs):
    @pl.when(pl.program_id(0) == 0)
    def _():
        for ref in refs:
            ref[...] = jnp.zeros_like(ref)


def first_kernel(pos_ref, base_ref, own_ref, mate_ref, got_ref, gotm_ref, e0, e1, e2, e3, w_ref, ah_ref,
                 u_ref, pairs, zs, zf, xs, ts, ss, ys, acc):
    planes = own_ref.shape[0]
    count = e0.shape[2]
    rows = count // HALF
    clear(pairs, zs, zf, xs, ss, acc)

    @pl.when(pl.program_id(0) == 0)
    def _():
        for part, (src, got) in enumerate(((own_ref, got_ref), (mate_ref, gotm_ref))):
            for k in range(planes):
                for half in range(2):

                    @pl.when(pos_ref[0] == half)
                    def _():
                        pairs[planes * part + k, :, :HALF] = src[k, :, HALF * half : HALF * (half + 1)]

                for fold in range(2):
                    pairs[planes * part + k, FOLD * fold : FOLD * fold + LINK, HALF : 2 * HALF] = got[
                        LINK * fold : LINK * (fold + 1), HALF * k : HALF * (k + 1)
                    ]

    for k, piece in enumerate((e0, e1, e2, e3)):
        start = rows * ((2 * pos_ref[0] + pos_ref[1]) ^ k)
        for row in range(rows):
            seg = piece[0, :, HALF * row : HALF * (row + 1)]
            y = start + row
            at = jnp.where(y <= NY // 2, y, FOLD + NY - y)
            for r in range(2):
                zf[r, pl.ds(at, 1), :] = seg[r : r + 1]
    for r in range(2):
        zs[r, :, :HALF] = zf[r]
        zs[r, :, HALF : 2 * HALF] = zf[r]
    normal(pairs, zs, w_ref, ah_ref, xs, ts, ss, ys, acc)
    for r in range(2):
        u_ref[0, r] = zf[r] - 0.5 * (acc[r, :, :HALF] + acc[r, :, HALF : 2 * HALF])


def pair_scratch():
    return [
        pltpu.VMEM((2, ROWS, LANES), F32),
        pltpu.VMEM((2, ROWS, HALF), F32),
        pltpu.VMEM((ROWS, 2 * GROUP * LANES), F32),
        pltpu.VMEM((LPAD, 2 * GROUP * LANES), F32),
        pltpu.VMEM((BACK, 2 * GROUP * LANES), BF),
        pltpu.VMEM((ROWS, 2 * GROUP * LANES), F32),
        pltpu.VMEM((2, ROWS, LANES), F32),
    ]


def line_specs():
    return [
        pl.BlockSpec((1, LPAD, ROWS), lambda d, p, s: (s[0] + d, 0, 0)),
        pl.BlockSpec((1, ROWS, BACK), lambda d, p, s: (s[0] + d, 0, 0)),
    ]


def first_step(pos, base, own, mate, got, gotm, pieces, w, ah):
    planes = own.shape[0]
    dirs, _, count = pieces[0].shape
    piece = pl.BlockSpec((1, 2, count), lambda d, p, s: (d, 0, 0))
    return pl.pallas_call(
        first_kernel,
        grid_spec=pltpu.PrefetchScalarGridSpec(
            num_scalar_prefetch=2,
            grid=(dirs,),
            in_specs=[whole(own.shape)] * 2 + [whole(got.shape)] * 2 + [piece] * 4 + line_specs(),
            out_specs=[
                pl.BlockSpec((1, 2, ROWS, HALF), lambda d, p, s: (d, 0, 0, 0)),
                result((2 * planes, ROWS, LANES)),
            ],
            scratch_shapes=pair_scratch(),
        ),
        out_shape=[
            jax.ShapeDtypeStruct((dirs, 2, ROWS, HALF), F32),
            jax.ShapeDtypeStruct((2 * planes, ROWS, LANES), F32),
        ],
        compiler_params=params(46),
        cost_estimate=cost(9e9, 30e6),
        name="first_step",
    )(pos, base, own, mate, got, gotm, *pieces, w, ah)


def second_kernel(pos_ref, base_ref, u_ref, keep_ref, got_ref, pairs, w_ref, ah_ref, z_ref, zs, zf, xs, ts, ss, ys, acc):
    clear(zs, zf, xs, ss, acc)
    for k in range(got_ref.shape[1] // (2 * HALF)):

        @pl.when(pl.program_id(0) == k)
        def _():
            for r in range(2):
                for part in range(2):
                    at = slice(FOLD * part, FOLD * part + LINK)
                    got = got_ref[LINK * part : LINK * (part + 1), HALF * (2 * k + r) : HALF * (2 * k + r + 1)]
                    zf[r, at, :] = 0.5 * (keep_ref[0, r, at, :] + got)

    for r in range(2):
        z = u_ref[0, r] + zf[r]
        zs[r, :, :HALF] = z
        zs[r, :, HALF : 2 * HALF] = z
        zf[r] = z + zf[r]
    normal(pairs, zs, w_ref, ah_ref, xs, ts, ss, ys, acc)
    for r in range(2):
        z_ref[0, r] = zf[r] - 0.5 * (acc[r, :, :HALF] + acc[r, :, HALF : 2 * HALF])


def second_step(pos, base, u, keep, got, pairs, w, ah):
    dirs = u.shape[0]
    plane = pl.BlockSpec((1, 2, ROWS, HALF), lambda d, p, s: (d, 0, 0, 0))
    return pl.pallas_call(
        second_kernel,
        grid_spec=pltpu.PrefetchScalarGridSpec(
            num_scalar_prefetch=2,
            grid=(dirs,),
            in_specs=[plane, plane, whole(got.shape), whole(pairs.shape)] + line_specs(),
            out_specs=plane,
            scratch_shapes=pair_scratch(),
        ),
        out_shape=jax.ShapeDtypeStruct(u.shape, F32),
        compiler_params=params(36),
        cost_estimate=cost(9e9, 20e6),
        name="second_step",
    )(pos, base, u, keep, got, pairs, w, ah)


def chunk_size(dirs):
    return -(-(75 * HALF) // (dirs * 128)) * 128


def flat_kernel(size, z_ref, o_ref, flat):
    dirs = z_ref.shape[0]
    rows = NY // 4
    parts = o_ref.shape[0] // 4
    for p in range(4):
        for row in range(rows):
            for d in range(dirs):
                for r in range(2):
                    at = folded(rows * p + row)
                    flat[d, r : r + 1, HALF * row : HALF * (row + 1)] = z_ref[d, r, at : at + 1, :]
        for q in range(parts):
            o_ref[4 * q + p] = flat[:, :, size * q : size * (q + 1)]


def flat_chunks(z, parts):
    dirs = z.shape[0]
    size = chunk_size(parts)
    shape = (4 * parts, dirs, 2, size)
    return pl.pallas_call(
        functools.partial(flat_kernel, size),
        grid=(1,),
        in_specs=[whole(z.shape)],
        out_specs=result(shape),
        out_shape=jax.ShapeDtypeStruct(shape, F32),
        scratch_shapes=[pltpu.VMEM((dirs, 2, size * parts), F32)],
        compiler_params=params(16),
        cost_estimate=cost(1e6, 5e6),
        name="flat_chunks",
    )(z)


def denoise_kernel(x_ref, w1_ref, b1_ref, w2_ref, o_ref, xs):
    parts = x_ref.shape[0] // 4
    own, size = x_ref.shape[1], x_ref.shape[3]
    for q in range(parts):
        for y in range(2):
            for core in range(2):
                for d in range(own):
                    at = 4 * own * q + 2 * own * core + 2 * d
                    xs[at : at + 2, size * y : size * (y + 1)] = x_ref[4 * q + 2 * y + core, d]
    w1h, w1l = split(w1_ref[...])
    w2h, w2l = split(w2_ref[...])
    w1 = jnp.concatenate([w1h, w1h, w1l], axis=1)
    w2 = jnp.concatenate([w2h, w2h, w2l], axis=1)
    x = xs[...]
    hi, lo = split(x)
    hidden = dot(w1, jnp.concatenate([hi, lo, hi], axis=0)) + b1_ref[...]
    hi, lo = split(jnp.maximum(hidden, 0.0))
    noise = dot(w2, jnp.concatenate([hi, lo, hi], axis=0))
    xs[...] = x - 0.5 * noise
    for q in range(parts):
        for d in range(2 * own):
            at = 4 * own * q + 2 * d
            o_ref[q, d] = xs[at : at + 2, :]


def denoise(x, w1, b1, w2):
    parts, own, size = x.shape[0] // 4, x.shape[1], x.shape[3]
    shape = (parts, 2 * own, 2, 2 * size)
    return pl.pallas_call(
        denoise_kernel,
        grid=(1,),
        in_specs=[whole(x.shape), whole(w1.shape), whole(b1.shape), whole(w2.shape)],
        out_specs=result(shape),
        out_shape=jax.ShapeDtypeStruct(shape, F32),
        scratch_shapes=[pltpu.VMEM((4 * own * parts, 2 * size), F32)],
        compiler_params=params(24),
        cost_estimate=cost(1e9, 3e6),
        name="denoise",
    )(x, w1, b1, w2)


def rows_kernel(x_ref, o_ref, flat):
    parts, size = x_ref.shape[0], x_ref.shape[3] // 2
    rows = o_ref.shape[2] // NX
    for half in range(2):
        for q in range(parts):
            flat[:, :, size * q : size * (q + 1)] = x_ref[q, :, :, size * half : size * (half + 1)]
        for row in range(rows):
            at = NX * row + HALF * half
            o_ref[:, :, at : at + HALF] = flat[:, :, HALF * row : HALF * (row + 1)]


def flat_rows(x, count):
    parts, dirs, _, size = x.shape
    return pl.pallas_call(
        rows_kernel,
        grid=(1,),
        in_specs=[whole(x.shape)],
        out_specs=result((dirs, 2, count)),
        out_shape=jax.ShapeDtypeStruct((dirs, 2, count), F32),
        scratch_shapes=[pltpu.VMEM((dirs, 2, parts * size // 2), F32)],
        compiler_params=params(16),
        cost_estimate=cost(1e6, 3e6),
        name="flat_rows",
    )(x)


def paired(estimate, coil_maps, kspace, lines, first_weight, first_bias, second_weight):
    dirs, _, share = estimate.shape
    own_dirs = dirs // 2
    coils = coil_maps.shape[0]
    parts = lax.axis_size("dir")
    back, rows = host_tables()
    high, low = split_host(back)
    f_back = jnp.asarray(np.concatenate([high, low]))
    index = lax.axis_index("coil")
    pos = jnp.stack([index // 2, index % 2]).astype(jnp.int32)
    mine = (own_dirs * pos[1:2]).astype(jnp.int32)

    def swap(value, k):
        return lax.ppermute(value, "coil", [(p, p ^ k) for p in range(4)])

    k_own = kspace.transpose(0, 1, 2, 4, 3, 5).reshape(dirs, 2 * coils, kspace.shape[4], 1, NX)
    maps, half = folded_maps(pos, coil_maps.reshape(2 * coils, 1, NY, NX).transpose(0, 2, 1, 3))
    mate = swap(maps, 1)
    k_mate = swap(k_own, 1)
    pieces = estimate_pieces(pos, estimate)
    pieces = [pieces[k] if k == 0 else swap(pieces[k], k) for k in range(4)]
    got = swap(half, 2)
    w, ah = line_matrices(lines, rows)
    keep, send = back_sums(mine, pos, own_dirs, k_own, k_mate, maps, mate, f_back, ah)
    send, got, *pieces = lax.optimization_barrier((send, got, *pieces))
    got_b = swap(send, 2)
    gotm = swap(got, 1)
    u, pairs = first_step(pos, mine, maps, mate, got, gotm, pieces, w, ah)
    z = second_step(pos, mine, u, keep, got_b, pairs, w, ah)
    chunks = flat_chunks(z, parts)
    received = lax.all_to_all(chunks, ("dir", "coil"), split_axis=0, concat_axis=0, tiled=True)
    channels = first_bias.shape[0]
    w1 = first_weight.reshape(-1, channels).T
    w2 = second_weight.reshape(channels, -1).T
    result = denoise(received, w1, first_bias[:, None], w2)
    returned = lax.all_to_all(result, "dir", split_axis=0, concat_axis=0, tiled=True)
    return flat_rows(returned, share)


def transform_rows(index, length):
    columns = jnp.arange(length, dtype=jnp.int32)
    product = index[:, None] * columns[None, :] % length
    angle = 2.0 * math.pi / length * product.astype(jnp.float32)
    scale = 1.0 / math.sqrt(length)
    return (jnp.cos(angle) * scale, -jnp.sin(angle) * scale)


def data_gradient(image, coil_maps, kspace, chosen, cols_cos, cols_sin):
    highest = lax.Precision.HIGHEST
    lines_cos, lines_sin = transform_rows(chosen, NY)
    coil_real, coil_imag = (coil_maps[:, 0], coil_maps[:, 1])
    image_real, image_imag = (image[0][None], image[1][None])
    prod_real = coil_real * image_real - coil_imag * image_imag
    prod_imag = coil_real * image_imag + coil_imag * image_real
    rows_form = "ly,csyx->cslx"
    half_real = jnp.einsum(rows_form, lines_cos, prod_real, precision=highest) - jnp.einsum(
        rows_form, lines_sin, prod_imag, precision=highest
    )
    half_imag = jnp.einsum(rows_form, lines_cos, prod_imag, precision=highest) + jnp.einsum(
        rows_form, lines_sin, prod_real, precision=highest
    )
    cols_form = "cslx,xk->cslk"
    pred_real = jnp.einsum(cols_form, half_real, cols_cos, precision=highest) - jnp.einsum(
        cols_form, half_imag, cols_sin, precision=highest
    )
    pred_imag = jnp.einsum(cols_form, half_real, cols_sin, precision=highest) + jnp.einsum(
        cols_form, half_imag, cols_cos, precision=highest
    )
    diff_real = pred_real - kspace[:, 0]
    diff_imag = pred_imag - kspace[:, 1]
    back_real = jnp.einsum(cols_form, diff_real, cols_cos, precision=highest) + jnp.einsum(
        cols_form, diff_imag, cols_sin, precision=highest
    )
    back_imag = jnp.einsum(cols_form, diff_imag, cols_cos, precision=highest) - jnp.einsum(
        cols_form, diff_real, cols_sin, precision=highest
    )
    adjoint_form = "ly,cslx->csyx"
    spread_real = jnp.einsum(adjoint_form, lines_cos, back_real, precision=highest) + jnp.einsum(
        adjoint_form, lines_sin, back_imag, precision=highest
    )
    spread_imag = jnp.einsum(adjoint_form, lines_cos, back_imag, precision=highest) - jnp.einsum(
        adjoint_form, lines_sin, back_real, precision=highest
    )
    grad_real = jnp.sum(coil_real * spread_real + coil_imag * spread_imag, axis=0)
    grad_imag = jnp.sum(coil_real * spread_imag - coil_imag * spread_real, axis=0)
    return jnp.stack([grad_real, grad_imag])


def per_device(estimate, coil_maps, kspace, lines, first_weight, first_bias, second_weight):
    highest = lax.Precision.HIGHEST
    dir_local = estimate.shape[0]
    share = estimate.shape[2]
    voxels = SLICES * NY * NX
    cols_cos, cols_sin = transform_rows(jnp.arange(NX, dtype=jnp.int32), NX)
    whole = lax.all_gather(estimate, "coil", axis=2, tiled=True)
    position = lax.axis_index("coil")
    current = whole
    for step in range(INNER):
        image = current.reshape(dir_local, 2, SLICES, NY, NX)

        def one_direction(item):
            return data_gradient(item[0], coil_maps, item[1], item[2], cols_cos, cols_sin)

        terms = lax.map(one_direction, (image, kspace, lines))
        total = lax.psum(terms.reshape(dir_local, 2, voxels), "coil")
        current = current - 0.5 * total
    own = lax.dynamic_slice_in_dim(current, position * share, share, 2)
    groups = lax.axis_size("dir")
    padded_len = -(-share // groups) * groups
    padded = jnp.pad(own, ((0, 0), (0, 0), (0, padded_len - share)))
    gathered = lax.all_to_all(padded, "dir", split_axis=2, concat_axis=0, tiled=True)
    hidden = (
        jnp.einsum("drv,drh->hv", gathered, first_weight, precision=highest) + first_bias[:, None]
    )
    hidden = jnp.maximum(hidden, 0.0)
    noise = jnp.einsum("hv,hdr->drv", hidden, second_weight, precision=highest)
    returned = lax.all_to_all(noise, "dir", split_axis=0, concat_axis=2, tiled=True)
    return own - 0.5 * returned[:, :, :share]


def chosen(*arrays):
    estimate, coil_maps, kspace = arrays[:3]
    fits = (
        lax.axis_size("coil") == 4
        and estimate.shape[0] % 2 == 0
        and estimate.shape[2] * 4 == NY * NX
        and coil_maps.shape[0] % 2 == 0
        and kspace.shape[4] <= LPAD
    )
    return paired(*arrays) if fits else per_device(*arrays)


def solution(mesh):
    return jax.shard_map(
        chosen,
        mesh=mesh,
        in_specs=(
            P("dir", None, "coil"),
            P("coil", None, None, None, None),
            P("dir", "coil", None, None, None, None),
            P("dir", None),
            P(),
            P(),
            P(),
        ),
        out_specs=P("dir", None, "coil"),
        check_vma=False,
    )
```

```python
import functools
import math

import jax
import jax.numpy as jnp
import ml_dtypes
import numpy as np
from jax import lax
from jax.experimental import pallas as pl
from jax.experimental.pallas import tpu as pltpu
from jax.sharding import PartitionSpec as P

NY = 300
NX = 300
INNER = 2
SLICES = 1
BF = jnp.bfloat16
F32 = jnp.float32
FOLD = 160
LINK = 152
ROWS = 2 * FOLD
LANES = 384
LPAD = 80
HALF = 150
BACK = 256
GROUP = 2


def split_host(table):
    high = table.astype(ml_dtypes.bfloat16)
    low = (table - high.astype(np.float64)).astype(ml_dtypes.bfloat16)
    return high, low


def host_tables():
    index = np.outer(np.arange(NX), np.arange(NX)) % NX
    angle = 2.0 * np.pi / NX * index
    cos, sin = np.cos(angle) / np.sqrt(NX), np.sin(angle) / np.sqrt(NX)
    back = np.zeros((2 * LANES, 2 * LANES))
    back[:NX, :NX] = cos
    back[LANES : LANES + NX, :NX] = -sin
    back[:NX, LANES : LANES + NX] = sin
    back[LANES : LANES + NX, LANES : LANES + NX] = cos
    rows = np.zeros((NY, ROWS))
    rows[:, : NY // 2 + 1] = cos[:, : NY // 2 + 1]
    rows[:, FOLD : FOLD + NY // 2] = sin[:, : NY // 2]
    return back, rows


def folded(row):
    return row if row <= NY // 2 else FOLD + NY - row


def split(value):
    high = value.astype(BF)
    return high, (value - high.astype(F32)).astype(BF)


def dot(a, b):
    return lax.dot_general(a, b, (((1,), (0,)), ((), ())), preferred_element_type=F32)


def dot_high(a, b, contract=(1, 0), precision=lax.Precision.HIGH):
    dims = (((contract[0],), (contract[1],)), ((), ()))
    return lax.dot_general(a, b, dims, precision=precision, preferred_element_type=F32)


def params(mib):
    return pltpu.CompilerParams(vmem_limit_bytes=mib * 2**20)


def cost(flops, nbytes):
    return pl.CostEstimate(flops=int(flops / 1000), bytes_accessed=int(nbytes / 1000), transcendentals=0)


def result(shape):
    return pl.BlockSpec(shape, lambda *_: (0,) * len(shape))


def whole(shape):
    return pl.BlockSpec(shape, lambda *_: (0,) * len(shape), pipeline_mode=pl.Buffered(1))


def lines_kernel(lines_ref, rows_ref, cols_ref, w_ref, ah_ref):
    pick = (lines_ref[0] == lax.broadcasted_iota(jnp.int32, (LPAD, NY), 1)).astype(F32)
    w_ref[0] = dot_high(pick, rows_ref[...], precision=lax.Precision.HIGHEST)
    hi, lo = split(dot_high(cols_ref[...], pick, (1, 1), precision=lax.Precision.HIGHEST))
    ah_ref[0] = jnp.concatenate(
        [v.astype(F32) for v in (hi, hi, lo)] + [jnp.zeros((ROWS, BACK - 3 * LPAD), F32)], axis=1
    ).astype(BF)


def line_matrices(lines, table):
    dirs, count = lines.shape
    padded = jnp.pad(lines, ((0, 0), (0, LPAD - count)), constant_values=-1)[:, :, None]
    tables = [jnp.asarray(t, F32) for t in (table, table.T)]
    return pl.pallas_call(
        lines_kernel,
        grid=(dirs,),
        in_specs=[pl.BlockSpec((1, LPAD, 1), lambda d: (d, 0, 0))] + [whole(t.shape) for t in tables],
        out_specs=[
            pl.BlockSpec((1, LPAD, ROWS), lambda d: (d, 0, 0)),
            pl.BlockSpec((1, ROWS, BACK), lambda d: (d, 0, 0)),
        ],
        out_shape=[
            jax.ShapeDtypeStruct((dirs, LPAD, ROWS), F32),
            jax.ShapeDtypeStruct((dirs, ROWS, BACK), BF),
        ],
        compiler_params=params(16),
        cost_estimate=cost(1e9, 1e6),
        name="line_matrices",
    )(padded, *tables)


def maps_kernel(pos_ref, maps_ref, out_ref, send_ref):
    planes = maps_ref.shape[0]
    mirror = FOLD + NY // 2
    send_ref[...] = jnp.zeros_like(send_ref)

    @pl.loop(0, planes)
    def _(k):
        out_ref[k] = jnp.zeros_like(out_ref[k])
        for row in range(NY):
            out_ref[k, folded(row), :NX] = maps_ref[k, row, 0, :]

    for half in range(2):

        @pl.when(pos_ref[0] != half)
        def _():
            for k in range(planes):
                for part in range(2):
                    send_ref[LINK * part : LINK * (part + 1), HALF * k : HALF * (k + 1)] = out_ref[
                        k, FOLD * part : FOLD * part + LINK, HALF * half : HALF * (half + 1)
                    ]


def folded_maps(pos, maps):
    planes = maps.shape[0]
    shapes = [(planes, ROWS, LANES), (2 * LINK, planes * HALF)]
    return pl.pallas_call(
        maps_kernel,
        grid_spec=pltpu.PrefetchScalarGridSpec(
            num_scalar_prefetch=1,
            grid=(1,),
            in_specs=[whole(maps.shape)],
            out_specs=[result(s) for s in shapes],
        ),
        out_shape=[jax.ShapeDtypeStruct(s, F32) for s in shapes],
        compiler_params=params(24),
        cost_estimate=cost(1e6, 12e6),
        name="folded_maps",
    )(pos, maps)


def estimate_kernel(pos_ref, est_ref, *out_refs):
    dirs, _, count = est_ref.shape
    own = dirs // 2
    rows = count // NX
    for y in range(2):

        @pl.when(pos_ref[0] == y)
        def _():
            for k, out_ref in enumerate(out_refs):
                group = pl.ds(own * (pos_ref[1] ^ (k % 2)), own)
                for row in range(rows):
                    at = NX * row + HALF * (y ^ (k // 2))
                    out_ref[:, :, HALF * row : HALF * (row + 1)] = est_ref[group, :, at : at + HALF]


def estimate_pieces(pos, estimate):
    dirs, _, count = estimate.shape
    shape = (dirs // 2, 2, count // 2)
    return pl.pallas_call(
        estimate_kernel,
        grid_spec=pltpu.PrefetchScalarGridSpec(
            num_scalar_prefetch=1,
            grid=(1,),
            in_specs=[whole(estimate.shape)],
            out_specs=[result(shape)] * 4,
        ),
        out_shape=[jax.ShapeDtypeStruct(shape, F32)] * 4,
        compiler_params=params(16),
        cost_estimate=cost(1e6, 8e6),
        name="estimate_pieces",
    )(pos, estimate)


def adjoint(y, j, rows):
    re, im = slice(2 * LANES * j, 2 * LANES * j + LANES), slice(2 * LANES * j + LANES, 2 * LANES * (j + 1))
    mirror = pl.ds(FOLD + rows.start, rows.size)
    ure, uim, vre, vim = y[rows, re], y[rows, im], y[mirror, re], y[mirror, im]
    return ((rows, ure - vim, uim + vre), (mirror, ure + vim, uim - vre))


def back_kernel(base_ref, pos_ref, k0_ref, k1_ref, c0_ref, c1_ref, f_ref, ah_ref, keep_ref, send_ref, xs, ss, ys, bs):
    coils = c0_ref.shape[0] // 2
    count = k0_ref.shape[2]
    wide = 2 * LANES

    @pl.when(pl.program_id(0) == 0)
    def _():
        xs[...] = jnp.zeros_like(xs)
        ss[...] = jnp.zeros_like(ss)

    def load(part, k_ref):
        for c in range(coils):
            for r in range(2):
                xs[part, LPAD * c : LPAD * c + count, LANES * r : LANES * r + NX] = k_ref[0, 2 * c + r, :, 0, :]

    def multiply(part):
        hi, lo = split(xs[part])
        t = dot(hi, f_ref[:wide]) + dot(lo, f_ref[:wide]) + dot(hi, f_ref[wide:])
        for c in range(coils):
            hi, lo = split(t[LPAD * c : LPAD * (c + 1)])
            lanes = slice(wide * c, wide * (c + 1))
            ss[part, :LPAD, lanes] = hi
            ss[part, LPAD : 2 * LPAD, lanes] = lo
            ss[part, 2 * LPAD : 3 * LPAD, lanes] = hi
        ys[part] = dot(ah_ref[0], ss[part])

    def gather(part, c_ref):
        for start in range(0, FOLD, 8):
            sums = [None] * 4
            if part > 0:
                sums = [bs[r, FOLD * f + start : FOLD * f + start + 8] for f in range(2) for r in range(2)]
            for c in range(coils):
                for f, (at, yre, yim) in enumerate(adjoint(ys.at[part], c, pl.ds(start, 8))):
                    cre, cim = c_ref[2 * c, at], c_ref[2 * c + 1, at]
                    for r, term in enumerate((cre * yre + cim * yim, cre * yim - cim * yre)):
                        old = sums[2 * f + r]
                        sums[2 * f + r] = term if old is None else old + term
            for f in range(2):
                for r in range(2):
                    bs[r, FOLD * f + start : FOLD * f + start + 8] = sums[2 * f + r]

    load(0, k0_ref)
    load(1, k1_ref)
    multiply(0)
    multiply(1)
    gather(0, c0_ref)
    gather(1, c1_ref)
    for half in range(2):
        lanes = slice(HALF * half, HALF * (half + 1))

        @pl.when(pos_ref[0] == half)
        def _():
            for r in range(2):
                keep_ref[0, r] = bs[r, :, lanes]

        for k in range(send_ref.shape[1] // (2 * HALF)):

            @pl.when((pos_ref[0] != half) & (pl.program_id(0) == k))
            def _():
                for r in range(2):
                    place = slice(HALF * (2 * k + r), HALF * (2 * k + r + 1))
                    for part in range(2):
                        send_ref[LINK * part : LINK * (part + 1), place] = bs[
                            r, FOLD * part : FOLD * part + LINK, lanes
                        ]


def back_sums(base, pos, dirs, k_own, k_mate, own, mate, f_back, ah):
    _, planes, count, _, _ = k_own.shape
    link = (2 * LINK, 2 * dirs * HALF)
    k_spec = pl.BlockSpec((1, planes, count, 1, NX), lambda d, s, *_: (s[0] + d, 0, 0, 0, 0))
    return pl.pallas_call(
        back_kernel,
        grid_spec=pltpu.PrefetchScalarGridSpec(
            num_scalar_prefetch=2,
            grid=(dirs,),
            in_specs=[k_spec] * 2
            + [whole((planes, ROWS, LANES))] * 2
            + [whole(f_back.shape), pl.BlockSpec((1, ROWS, BACK), lambda d, s, *_: (s[0] + d, 0, 0))],
            out_specs=[pl.BlockSpec((1, 2, ROWS, HALF), lambda d, *_: (d, 0, 0, 0)), result(link)],
            scratch_shapes=[
                pltpu.VMEM((2, planes // 2 * LPAD, 2 * LANES), F32),
                pltpu.VMEM((2, BACK, planes * LANES), BF),
                pltpu.VMEM((2, ROWS, planes * LANES), F32),
                pltpu.VMEM((2, ROWS, LANES), F32),
            ],
        ),
        out_shape=[jax.ShapeDtypeStruct((dirs, 2, ROWS, HALF), F32), jax.ShapeDtypeStruct(link, F32)],
        compiler_params=params(48),
        cost_estimate=cost(14e9, 22e6),
        name="back_sums",
    )(base, pos, k_own, k_mate, own, mate, f_back, ah)


def normal(pairs, zs, w_ref, ah_ref, xs, ss, ys, acc):
    groups = pairs.shape[0] // (2 * GROUP)
    wide = 2 * LANES

    def products(g):
        x = xs.at[g % 2]
        for at in range(0, FOLD, 8):
            rows = (slice(at, at + 8), slice(FOLD + at, FOLD + at + 8))
            for lane in range(0, LANES, 128):
                lanes = slice(lane, lane + 128)
                z = [(zs[0, r, lanes], zs[1, r, lanes]) for r in rows]
                for j in range(GROUP):
                    p = 2 * (GROUP * g + j)
                    parts = []
                    for (zre, zim), r in zip(z, rows):
                        cre, cim = pairs[p, r, lanes], pairs[p + 1, r, lanes]
                        parts.append((cre * zre - cim * zim, cre * zim + cim * zre))
                    (re1, im1), (re2, im2) = parts
                    put = slice(wide * j + lane, wide * j + lane + 128)
                    x[rows[0], put] = re1 + re2
                    x[rows[1], put] = im1 - im2
                    put = slice(put.start + LANES, put.stop + LANES)
                    x[rows[0], put] = im1 + im2
                    x[rows[1], put] = re2 - re1

    def multiply(g):
        s = ss.at[g % 2]
        hi, lo = split(dot_high(w_ref[0], xs[g % 2]))
        s[:LPAD] = hi
        s[LPAD : 2 * LPAD] = lo
        s[2 * LPAD : 3 * LPAD] = hi
        ys[g % 2] = dot(ah_ref[0], s[...])

    def gather(g):
        for at in range(0, FOLD, 8):
            rows = (slice(at, at + 8), slice(FOLD + at, FOLD + at + 8))
            for lane in range(0, LANES, 128):
                lanes = slice(lane, lane + 128)
                sums = [None] * 4
                if g > 0:
                    sums = [acc[r, rows[part], lanes] for part in range(2) for r in range(2)]
                for j in range(GROUP):
                    p = 2 * (GROUP * g + j)
                    re = slice(wide * j + lane, wide * j + lane + 128)
                    im = slice(re.start + LANES, re.stop + LANES)
                    ure, uim = ys[g % 2, rows[0], re], ys[g % 2, rows[0], im]
                    vre, vim = ys[g % 2, rows[1], re], ys[g % 2, rows[1], im]
                    for part, (yre, yim) in enumerate(((ure - vim, uim + vre), (ure + vim, uim - vre))):
                        cre, cim = pairs[p, rows[part], lanes], pairs[p + 1, rows[part], lanes]
                        for r, term in enumerate((cre * yre + cim * yim, cre * yim - cim * yre)):
                            old = sums[2 * part + r]
                            sums[2 * part + r] = term if old is None else old + term
                for part in range(2):
                    for r in range(2):
                        acc[r, rows[part], lanes] = sums[2 * part + r]

    for g in range(groups + 2):
        if g < groups:
            products(g)
        if 1 <= g <= groups:
            multiply(g - 1)
        if g >= 2:
            gather(g - 2)


def clear(*refs):
    @pl.when(pl.program_id(0) == 0)
    def _():
        for ref in refs:
            ref[...] = jnp.zeros_like(ref)


def first_kernel(pos_ref, base_ref, own_ref, mate_ref, got_ref, gotm_ref, e0, e1, e2, e3, w_ref, ah_ref,
                 u_ref, pairs, zs, zf, xs, ss, ys, acc):
    planes = own_ref.shape[0]
    count = e0.shape[2]
    rows = count // HALF
    clear(pairs, zs, zf, ss)

    @pl.when(pl.program_id(0) == 0)
    def _():
        for part, (src, got) in enumerate(((own_ref, got_ref), (mate_ref, gotm_ref))):
            for k in range(planes):
                for half in range(2):

                    @pl.when(pos_ref[0] == half)
                    def _():
                        pairs[planes * part + k, :, :HALF] = src[k, :, HALF * half : HALF * (half + 1)]

                for fold in range(2):
                    pairs[planes * part + k, FOLD * fold : FOLD * fold + LINK, HALF : 2 * HALF] = got[
                        LINK * fold : LINK * (fold + 1), HALF * k : HALF * (k + 1)
                    ]

    for k, piece in enumerate((e0, e1, e2, e3)):
        start = rows * ((2 * pos_ref[0] + pos_ref[1]) ^ k)
        for row in range(rows):
            seg = piece[0, :, HALF * row : HALF * (row + 1)]
            y = start + row
            at = jnp.where(y <= NY // 2, y, FOLD + NY - y)
            for r in range(2):
                zf[r, pl.ds(at, 1), :] = seg[r : r + 1]
    for r in range(2):
        zs[r, :, :HALF] = zf[r]
        zs[r, :, HALF : 2 * HALF] = zf[r]
    normal(pairs, zs, w_ref, ah_ref, xs, ss, ys, acc)
    for r in range(2):
        u_ref[0, r] = zf[r] - 0.5 * (acc[r, :, :HALF] + acc[r, :, HALF : 2 * HALF])


def pair_scratch():
    return [
        pltpu.VMEM((2, ROWS, LANES), F32),
        pltpu.VMEM((2, ROWS, HALF), F32),
        pltpu.VMEM((2, ROWS, 2 * GROUP * LANES), F32),
        pltpu.VMEM((2, BACK, 2 * GROUP * LANES), BF),
        pltpu.VMEM((2, ROWS, 2 * GROUP * LANES), F32),
        pltpu.VMEM((2, ROWS, LANES), F32),
    ]


def line_specs():
    return [
        pl.BlockSpec((1, LPAD, ROWS), lambda d, p, s: (s[0] + d, 0, 0)),
        pl.BlockSpec((1, ROWS, BACK), lambda d, p, s: (s[0] + d, 0, 0)),
    ]


def first_step(pos, base, own, mate, got, gotm, pieces, w, ah):
    planes = own.shape[0]
    dirs, _, count = pieces[0].shape
    piece = pl.BlockSpec((1, 2, count), lambda d, p, s: (d, 0, 0))
    return pl.pallas_call(
        first_kernel,
        grid_spec=pltpu.PrefetchScalarGridSpec(
            num_scalar_prefetch=2,
            grid=(dirs,),
            in_specs=[whole(own.shape)] * 2 + [whole(got.shape)] * 2 + [piece] * 4 + line_specs(),
            out_specs=[
                pl.BlockSpec((1, 2, ROWS, HALF), lambda d, p, s: (d, 0, 0, 0)),
                result((2 * planes, ROWS, LANES)),
            ],
            scratch_shapes=pair_scratch(),
        ),
        out_shape=[
            jax.ShapeDtypeStruct((dirs, 2, ROWS, HALF), F32),
            jax.ShapeDtypeStruct((2 * planes, ROWS, LANES), F32),
        ],
        compiler_params=params(46),
        cost_estimate=cost(9e9, 30e6),
        name="first_step",
    )(pos, base, own, mate, got, gotm, *pieces, w, ah)


def second_kernel(pos_ref, base_ref, u_ref, keep_ref, got_ref, pairs, w_ref, ah_ref, z_ref, zs, zf, xs, ss, ys, acc):
    clear(zs, zf, ss)
    for k in range(got_ref.shape[1] // (2 * HALF)):

        @pl.when(pl.program_id(0) == k)
        def _():
            for r in range(2):
                for part in range(2):
                    at = slice(FOLD * part, FOLD * part + LINK)
                    got = got_ref[LINK * part : LINK * (part + 1), HALF * (2 * k + r) : HALF * (2 * k + r + 1)]
                    zf[r, at, :] = 0.5 * (keep_ref[0, r, at, :] + got)

    for r in range(2):
        z = u_ref[0, r] + zf[r]
        zs[r, :, :HALF] = z
        zs[r, :, HALF : 2 * HALF] = z
        zf[r] = z + zf[r]
    normal(pairs, zs, w_ref, ah_ref, xs, ss, ys, acc)
    for r in range(2):
        z_ref[0, r] = zf[r] - 0.5 * (acc[r, :, :HALF] + acc[r, :, HALF : 2 * HALF])


def second_step(pos, base, u, keep, got, pairs, w, ah):
    dirs = u.shape[0]
    plane = pl.BlockSpec((1, 2, ROWS, HALF), lambda d, p, s: (d, 0, 0, 0))
    return pl.pallas_call(
        second_kernel,
        grid_spec=pltpu.PrefetchScalarGridSpec(
            num_scalar_prefetch=2,
            grid=(dirs,),
            in_specs=[plane, plane, whole(got.shape), whole(pairs.shape)] + line_specs(),
            out_specs=plane,
            scratch_shapes=pair_scratch(),
        ),
        out_shape=jax.ShapeDtypeStruct(u.shape, F32),
        compiler_params=params(36),
        cost_estimate=cost(9e9, 20e6),
        name="second_step",
    )(pos, base, u, keep, got, pairs, w, ah)


def chunk_size(dirs):
    return -(-(75 * HALF) // (dirs * 128)) * 128


def flat_kernel(size, z_ref, o_ref, flat):
    dirs = z_ref.shape[0]
    rows = NY // 4
    parts = o_ref.shape[0] // 4
    for p in range(4):
        for row in range(rows):
            for d in range(dirs):
                for r in range(2):
                    at = folded(rows * p + row)
                    flat[d, r : r + 1, HALF * row : HALF * (row + 1)] = z_ref[d, r, at : at + 1, :]
        for q in range(parts):
            o_ref[4 * q + p] = flat[:, :, size * q : size * (q + 1)]


def flat_chunks(z, parts):
    dirs = z.shape[0]
    size = chunk_size(parts)
    shape = (4 * parts, dirs, 2, size)
    return pl.pallas_call(
        functools.partial(flat_kernel, size),
        grid=(1,),
        in_specs=[whole(z.shape)],
        out_specs=result(shape),
        out_shape=jax.ShapeDtypeStruct(shape, F32),
        scratch_shapes=[pltpu.VMEM((dirs, 2, size * parts), F32)],
        compiler_params=params(16),
        cost_estimate=cost(1e6, 5e6),
        name="flat_chunks",
    )(z)


def denoise_kernel(x_ref, w1_ref, b1_ref, w2_ref, o_ref, xs):
    parts = x_ref.shape[0] // 4
    own, size = x_ref.shape[1], x_ref.shape[3]
    for q in range(parts):
        for y in range(2):
            for core in range(2):
                for d in range(own):
                    at = 4 * own * q + 2 * own * core + 2 * d
                    xs[at : at + 2, size * y : size * (y + 1)] = x_ref[4 * q + 2 * y + core, d]
    w1h, w1l = split(w1_ref[...])
    w2h, w2l = split(w2_ref[...])
    w1 = jnp.concatenate([w1h, w1h, w1l], axis=1)
    w2 = jnp.concatenate([w2h, w2h, w2l], axis=1)
    x = xs[...]
    hi, lo = split(x)
    hidden = dot(w1, jnp.concatenate([hi, lo, hi], axis=0)) + b1_ref[...]
    hi, lo = split(jnp.maximum(hidden, 0.0))
    noise = dot(w2, jnp.concatenate([hi, lo, hi], axis=0))
    xs[...] = x - 0.5 * noise
    for q in range(parts):
        for d in range(2 * own):
            at = 4 * own * q + 2 * d
            o_ref[q, d] = xs[at : at + 2, :]


def denoise(x, w1, b1, w2):
    parts, own, size = x.shape[0] // 4, x.shape[1], x.shape[3]
    shape = (parts, 2 * own, 2, 2 * size)
    return pl.pallas_call(
        denoise_kernel,
        grid=(1,),
        in_specs=[whole(x.shape), whole(w1.shape), whole(b1.shape), whole(w2.shape)],
        out_specs=result(shape),
        out_shape=jax.ShapeDtypeStruct(shape, F32),
        scratch_shapes=[pltpu.VMEM((4 * own * parts, 2 * size), F32)],
        compiler_params=params(24),
        cost_estimate=cost(1e9, 3e6),
        name="denoise",
    )(x, w1, b1, w2)


def rows_kernel(x_ref, o_ref, flat):
    parts, size = x_ref.shape[0], x_ref.shape[3] // 2
    rows = o_ref.shape[2] // NX
    for half in range(2):
        for q in range(parts):
            flat[:, :, size * q : size * (q + 1)] = x_ref[q, :, :, size * half : size * (half + 1)]
        for row in range(rows):
            at = NX * row + HALF * half
            o_ref[:, :, at : at + HALF] = flat[:, :, HALF * row : HALF * (row + 1)]


def flat_rows(x, count):
    parts, dirs, _, size = x.shape
    return pl.pallas_call(
        rows_kernel,
        grid=(1,),
        in_specs=[whole(x.shape)],
        out_specs=result((dirs, 2, count)),
        out_shape=jax.ShapeDtypeStruct((dirs, 2, count), F32),
        scratch_shapes=[pltpu.VMEM((dirs, 2, parts * size // 2), F32)],
        compiler_params=params(16),
        cost_estimate=cost(1e6, 3e6),
        name="flat_rows",
    )(x)


def paired(estimate, coil_maps, kspace, lines, first_weight, first_bias, second_weight):
    dirs, _, share = estimate.shape
    own_dirs = dirs // 2
    coils = coil_maps.shape[0]
    parts = lax.axis_size("dir")
    back, rows = host_tables()
    high, low = split_host(back)
    f_back = jnp.asarray(np.concatenate([high, low]))
    index = lax.axis_index("coil")
    pos = jnp.stack([index // 2, index % 2]).astype(jnp.int32)
    mine = (own_dirs * pos[1:2]).astype(jnp.int32)

    def swap(value, k):
        return lax.ppermute(value, "coil", [(p, p ^ k) for p in range(4)])

    k_own = kspace.transpose(0, 1, 2, 4, 3, 5).reshape(dirs, 2 * coils, kspace.shape[4], 1, NX)
    maps, half = folded_maps(pos, coil_maps.reshape(2 * coils, 1, NY, NX).transpose(0, 2, 1, 3))
    mate = swap(maps, 1)
    k_mate = swap(k_own, 1)
    pieces = estimate_pieces(pos, estimate)
    pieces = [pieces[k] if k == 0 else swap(pieces[k], k) for k in range(4)]
    got = swap(half, 2)
    w, ah = line_matrices(lines, rows)
    keep, send = back_sums(mine, pos, own_dirs, k_own, k_mate, maps, mate, f_back, ah)
    send, got, *pieces = lax.optimization_barrier((send, got, *pieces))
    got_b = swap(send, 2)
    gotm = swap(got, 1)
    u, pairs = first_step(pos, mine, maps, mate, got, gotm, pieces, w, ah)
    z = second_step(pos, mine, u, keep, got_b, pairs, w, ah)
    chunks = flat_chunks(z, parts)
    received = lax.all_to_all(chunks, ("dir", "coil"), split_axis=0, concat_axis=0, tiled=True)
    channels = first_bias.shape[0]
    w1 = first_weight.reshape(-1, channels).T
    w2 = second_weight.reshape(channels, -1).T
    result = denoise(received, w1, first_bias[:, None], w2)
    returned = lax.all_to_all(result, "dir", split_axis=0, concat_axis=0, tiled=True)
    return flat_rows(returned, share)


def transform_rows(index, length):
    columns = jnp.arange(length, dtype=jnp.int32)
    product = index[:, None] * columns[None, :] % length
    angle = 2.0 * math.pi / length * product.astype(jnp.float32)
    scale = 1.0 / math.sqrt(length)
    return (jnp.cos(angle) * scale, -jnp.sin(angle) * scale)


def data_gradient(image, coil_maps, kspace, chosen, cols_cos, cols_sin):
    highest = lax.Precision.HIGHEST
    lines_cos, lines_sin = transform_rows(chosen, NY)
    coil_real, coil_imag = (coil_maps[:, 0], coil_maps[:, 1])
    image_real, image_imag = (image[0][None], image[1][None])
    prod_real = coil_real * image_real - coil_imag * image_imag
    prod_imag = coil_real * image_imag + coil_imag * image_real
    rows_form = "ly,csyx->cslx"
    half_real = jnp.einsum(rows_form, lines_cos, prod_real, precision=highest) - jnp.einsum(
        rows_form, lines_sin, prod_imag, precision=highest
    )
    half_imag = jnp.einsum(rows_form, lines_cos, prod_imag, precision=highest) + jnp.einsum(
        rows_form, lines_sin, prod_real, precision=highest
    )
    cols_form = "cslx,xk->cslk"
    pred_real = jnp.einsum(cols_form, half_real, cols_cos, precision=highest) - jnp.einsum(
        cols_form, half_imag, cols_sin, precision=highest
    )
    pred_imag = jnp.einsum(cols_form, half_real, cols_sin, precision=highest) + jnp.einsum(
        cols_form, half_imag, cols_cos, precision=highest
    )
    diff_real = pred_real - kspace[:, 0]
    diff_imag = pred_imag - kspace[:, 1]
    back_real = jnp.einsum(cols_form, diff_real, cols_cos, precision=highest) + jnp.einsum(
        cols_form, diff_imag, cols_sin, precision=highest
    )
    back_imag = jnp.einsum(cols_form, diff_imag, cols_cos, precision=highest) - jnp.einsum(
        cols_form, diff_real, cols_sin, precision=highest
    )
    adjoint_form = "ly,cslx->csyx"
    spread_real = jnp.einsum(adjoint_form, lines_cos, back_real, precision=highest) + jnp.einsum(
        adjoint_form, lines_sin, back_imag, precision=highest
    )
    spread_imag = jnp.einsum(adjoint_form, lines_cos, back_imag, precision=highest) - jnp.einsum(
        adjoint_form, lines_sin, back_real, precision=highest
    )
    grad_real = jnp.sum(coil_real * spread_real + coil_imag * spread_imag, axis=0)
    grad_imag = jnp.sum(coil_real * spread_imag - coil_imag * spread_real, axis=0)
    return jnp.stack([grad_real, grad_imag])


def per_device(estimate, coil_maps, kspace, lines, first_weight, first_bias, second_weight):
    highest = lax.Precision.HIGHEST
    dir_local = estimate.shape[0]
    share = estimate.shape[2]
    voxels = SLICES * NY * NX
    cols_cos, cols_sin = transform_rows(jnp.arange(NX, dtype=jnp.int32), NX)
    whole = lax.all_gather(estimate, "coil", axis=2, tiled=True)
    position = lax.axis_index("coil")
    current = whole
    for step in range(INNER):
        image = current.reshape(dir_local, 2, SLICES, NY, NX)

        def one_direction(item):
            return data_gradient(item[0], coil_maps, item[1], item[2], cols_cos, cols_sin)

        terms = lax.map(one_direction, (image, kspace, lines))
        total = lax.psum(terms.reshape(dir_local, 2, voxels), "coil")
        current = current - 0.5 * total
    own = lax.dynamic_slice_in_dim(current, position * share, share, 2)
    groups = lax.axis_size("dir")
    padded_len = -(-share // groups) * groups
    padded = jnp.pad(own, ((0, 0), (0, 0), (0, padded_len - share)))
    gathered = lax.all_to_all(padded, "dir", split_axis=2, concat_axis=0, tiled=True)
    hidden = (
        jnp.einsum("drv,drh->hv", gathered, first_weight, precision=highest) + first_bias[:, None]
    )
    hidden = jnp.maximum(hidden, 0.0)
    noise = jnp.einsum("hv,hdr->drv", hidden, second_weight, precision=highest)
    returned = lax.all_to_all(noise, "dir", split_axis=0, concat_axis=2, tiled=True)
    return own - 0.5 * returned[:, :, :share]


def chosen(*arrays):
    estimate, coil_maps, kspace = arrays[:3]
    fits = (
        lax.axis_size("coil") == 4
        and estimate.shape[0] % 2 == 0
        and estimate.shape[2] * 4 == NY * NX
        and coil_maps.shape[0] % 2 == 0
        and kspace.shape[4] <= LPAD
    )
    return paired(*arrays) if fits else per_device(*arrays)


def solution(mesh):
    return jax.shard_map(
        chosen,
        mesh=mesh,
        in_specs=(
            P("dir", None, "coil"),
            P("coil", None, None, None, None),
            P("dir", "coil", None, None, None, None),
            P("dir", None),
            P(),
            P(),
            P(),
        ),
        out_specs=P("dir", None, "coil"),
        check_vma=False,
    )
```
